32 devices in a mesh: groups: 2 (over y), patch: 8 (over z, x), head: 2 (over core).
Axes of the slice: x: 2, y: 2, z: 4, core: 2. Of those that a mesh axis runs over, the one named last changes fastest.
Arguments:
- tokens: bfloat16 [2048, 1536], P(('groups', 'patch', 'head')), parts along dimension 0, may hold values from -6 to 6
- timestep: int32 [2], P('groups'), parts along dimension 0, may hold values from 0 to 27
- text_length: int32 [2], P('groups'), parts along dimension 0, may hold values from 128 to 512
- mod_table: float32 [28, 3, 1536], replicated, may hold values from -4 to 4
- w_qkv: bfloat16 [1536, 3, 1536], P(None, None, 'head'), may hold values from -0.15625 to 0.15625
- q_gain: float32 [128], replicated, may hold values from 0.8 to 2
- k_gain: float32 [128], replicated, may hold values from 0.8 to 2
- w_out: bfloat16 [1536, 1536], replicated, may hold values from -0.15625 to 0.15625
- stale_kv: bfloat16 [2, 2048, 1536], P(None, ('groups', 'patch'), 'head'), parts along dimension 1, may hold values from -6 to 6
Outputs:
- update: bfloat16 [2048, 1536], P(('groups', 'patch', 'head')), parts along dimension 0
- new_kv: bfloat16 [2, 2048, 1536], P(None, ('groups', 'patch'), 'head'), parts along dimension 1
The draws below stay inside these ranges and needn't reach their ends.
There are 2 independent parts, one for each index of `groups`. The reference program is written for one: setup_inputs(seed, part) draws one part's arguments, and reference() takes and returns one part's arrays. A program takes and returns all parts, laid end to end along the dimension named above; an argument that names none is the same for every part. Nothing has to cross between parts.
All inputs are finite; a program needn't handle non-finite values.
Results may differ from the reference program's by a relative error of at most 0.0089.
The reference program's roundings to bfloat16 on the way (of `normed`, `queries`, `fresh_keys`, `fresh_values`, `rounded` and `attention`) count: a program that leaves them out, or rounds other values in their place, can miss the bound.
Values may be sent and summed in bfloat16 or wider, within the bound.
A program may use at most 128 MiB of HBM per device.

```python
import math
import jax
import jax.numpy as jnp
from jax import lax

D = 1536
HEADS = 12
HD = 128
STEPS = 28
TOK_DEV = 64
SEQ = 1024
TXT = 512
N_PATCH = 8
N_HEAD = 2


def block_levels(key, dims, pieces, low, high):
    gain, own = 1.0, jax.random.fold_in(key, 6)
    for axis_at, parts in pieces:
        steps = jnp.exp(jax.random.uniform(jax.random.fold_in(own, axis_at), (parts,), jnp.float32, low / len(pieces), high / len(pieces)))
        gain = gain * jnp.repeat(steps, dims[axis_at] // parts).reshape([-1 if axis == axis_at else 1 for axis in range(len(dims))])
    return gain


def bell_draw(key, extent, deviation, reach, pieces=(), kind=jnp.bfloat16):
    values = deviation * jax.random.normal(key, extent, jnp.float32)
    if pieces:
        values = values * block_levels(key, extent, pieces, -0.22, 0.18)
    return jnp.clip(values, -reach, reach).astype(kind)


def setup_inputs(seed: int = 0, part: int = 0) -> dict:
    key_of = jax.random.split(jax.random.key(seed), 10)
    part_splits = jax.random.split(jax.random.fold_in(key_of[9], part), 10)
    tokens = bell_draw(part_splits[0], (SEQ, D), 1.0, 6.0, ((0, 16),))
    timestep = jax.random.randint(part_splits[1], (1,), 0, STEPS).astype(jnp.int32)
    text_length = jax.random.randint(part_splits[2], (1,), TXT // 4, TXT + 1).astype(jnp.int32)
    mod_table = bell_draw(key_of[3], (STEPS, 3, D), 1.0, 4.0, (), jnp.float32)
    w_qkv = bell_draw(key_of[4], (D, 3, HEADS * HD), D ** -0.5, 0.15625, ((2, 2),))
    q_gain = jnp.clip(jnp.exp(jax.random.uniform(key_of[5], (HD,), jnp.float32, math.log(0.8), math.log(2.0))), 0.8, 2.0)
    k_gain = jnp.clip(jnp.exp(jax.random.uniform(key_of[6], (HD,), jnp.float32, math.log(0.8), math.log(2.0))), 0.8, 2.0)
    w_out = bell_draw(key_of[7], (HEADS * HD, D), (HEADS * HD) ** -0.5, 0.15625)
    stale_kv = bell_draw(part_splits[8], (2, SEQ, HEADS * HD), 1.0, 6.0, ((1, 8), (2, 2)))
    return dict(tokens=tokens, timestep=timestep, text_length=text_length, mod_table=mod_table, w_qkv=w_qkv, q_gain=q_gain, k_gain=k_gain, w_out=w_out, stale_kv=stale_kv)


epsilon = 1e-06

def rms_scaled(values, gain_vec):
    mean_square = lax.optimization_barrier(jnp.mean(values * values, axis=-1, keepdims=True))
    return (values * lax.rsqrt(mean_square + epsilon) * gain_vec).astype(jnp.bfloat16)

def reference(tokens, timestep, text_length, mod_table, w_qkv, q_gain, k_gain, w_out, stale_kv):
    sequence = TOK_DEV * N_PATCH * N_HEAD
    patch_rows = TOK_DEV * N_HEAD
    head_width = HEADS * HD
    modulation = lax.dynamic_index_in_dim(mod_table, timestep[0], 0, keepdims=False)
    shift_row, scale_row, gate_row = (modulation[0], modulation[1], modulation[2])
    widened = tokens.astype(jnp.float32)
    centred = widened - lax.optimization_barrier(jnp.mean(widened, axis=-1, keepdims=True))
    variance = lax.optimization_barrier(jnp.mean(centred * centred, axis=-1, keepdims=True))
    normed = (centred * lax.rsqrt(variance + epsilon) * (1.0 + scale_row) + shift_row).astype(jnp.bfloat16)
    mixed = jnp.dot(normed, w_qkv.reshape(D, 3 * head_width), preferred_element_type=jnp.float32)
    mixed = mixed.reshape(sequence, 3, HEADS, HD)
    queries = rms_scaled(mixed[:, 0], q_gain)
    fresh_keys = rms_scaled(mixed[:, 1], k_gain)
    fresh_values = mixed[:, 2].astype(jnp.bfloat16)
    new_kv = jnp.stack([fresh_keys.reshape(sequence, head_width), fresh_values.reshape(sequence, head_width)])
    old_keys = stale_kv[0].reshape(sequence, HEADS, HD)
    old_values = stale_kv[1].reshape(sequence, HEADS, HD)
    position = jnp.arange(sequence, dtype=jnp.int32)
    visible = ((position >= TXT) | (position < text_length[0])).astype(jnp.float32)
    inverse_root = 1.0 / math.sqrt(HD)

    def one_patch(patch_index):
        first_row = (patch_index * patch_rows).astype(jnp.int32)
        query_rows = lax.dynamic_slice_in_dim(queries, first_row, patch_rows, 0)
        key_rows = lax.dynamic_update_slice_in_dim(old_keys, lax.dynamic_slice_in_dim(fresh_keys, first_row, patch_rows, 0), first_row, 0)
        value_rows = lax.dynamic_update_slice_in_dim(old_values, lax.dynamic_slice_in_dim(fresh_values, first_row, patch_rows, 0), first_row, 0)
        scores = jnp.einsum('qhd,khd->hqk', query_rows.astype(jnp.float32), key_rows.astype(jnp.float32)) * inverse_root
        exps = jnp.exp(scores) * visible[None, None, :]
        denominator = lax.optimization_barrier(jnp.sum(exps, axis=-1))
        rounded = lax.optimization_barrier(exps.astype(jnp.bfloat16)).astype(jnp.float32)
        numerator = jnp.einsum('hqk,khd->qhd', rounded, value_rows.astype(jnp.float32))
        result = numerator / jnp.transpose(denominator)[:, :, None]
        return result.astype(jnp.bfloat16).reshape(patch_rows, head_width)
    attention = lax.map(one_patch, jnp.arange(N_PATCH, dtype=jnp.int32)).reshape(sequence, head_width)
    projected = jnp.dot(attention, w_out, preferred_element_type=jnp.float32)
    update = (gate_row * projected).astype(jnp.bfloat16)
    return (update, new_kv)
```

```python
import math

import jax
import jax.numpy as jnp
from jax import lax
from jax.experimental import pallas as pl
from jax.experimental.pallas import tpu as pltpu
from jax.sharding import PartitionSpec as P

HD = 128
epsilon = 1e-06
MESH = pl.DeviceIdType.MESH
ACROSS, DOWN, UP = 0, 1, 2


def rms_scaled(values, gain_vec):
    mean_square = jnp.mean(values * values, axis=-1, keepdims=True)
    return (values * lax.rsqrt(mean_square + epsilon) * gain_vec).astype(jnp.bfloat16)


def body(n_patch, timestep, length, tokens, mod, w_qkv, q_gain, k_gain, w_out, stale, update, new_kv,
         tok_v, mod_v, w_v, wo_v, rows_v, q_v, kv_v, far, num, den, att, att_in,
         local_sem, head_sem, send_sem, recv_sem):
    tok_dev = tokens.shape[0]
    patch_rows = 2 * tok_dev
    half_rows = patch_rows // 2
    width = w_qkv.shape[2]
    heads = width // HD
    text_rows = 4 * patch_rows
    n_z = n_patch // 2
    inverse_root = 1.0 / math.sqrt(HD)

    me = lax.axis_index("patch")
    core = lax.axis_index("head")
    z, x = lax.div(me, 2), lax.rem(me, 2)
    xp = 1 - x
    has_up, has_down = z < n_z - 1, z > 0
    targets = {ACROSS: 2 * z + xp, DOWN: me - 2, UP: me + 2}

    def local(src, dst, at):
        return pltpu.make_async_copy(src, dst, local_sem.at[at])

    loads = [local(tokens, tok_v, 0), local(mod, mod_v, 1)]
    loads += [local(w_qkv.at[i], w_v.at[i], 2 + i) for i in range(3)]
    loads += [local(w_out, wo_v, 5)]
    for load in loads:
        load.start()

    barrier = pltpu.get_barrier_semaphore()
    pl.semaphore_signal(barrier, inc=1, device_id={"head": 1 - core}, device_id_type=MESH)
    pl.semaphore_signal(barrier, inc=1, device_id={"patch": targets[ACROSS]}, device_id_type=MESH)

    @pl.when(has_up)
    def _():
        pl.semaphore_signal(barrier, inc=1, device_id={"patch": targets[UP]}, device_id_type=MESH)

    @pl.when(has_down)
    def _():
        pl.semaphore_signal(barrier, inc=1, device_id={"patch": targets[DOWN]}, device_id_type=MESH)

    pl.semaphore_wait(barrier, 2 + has_up.astype(jnp.int32) + has_down.astype(jnp.int32))

    def piece(p, half):
        return far.at[p, :, pl.ds(half * half_rows, half_rows), :]

    def send(p, half, way, own=False):
        src = stale.at[:, pl.ds(half * half_rows, half_rows), :] if own else piece(p, half)
        return pltpu.make_async_remote_copy(
            src_ref=src, dst_ref=piece(p, half),
            send_sem=send_sem.at[way, p, half], recv_sem=recv_sem.at[p, half],
            device_id={"patch": targets[way]}, device_id_type=MESH,
        )

    def own_sends(act):
        for half, zhalf in ((1, 0), (0, 1)):
            act(send(me, half, ACROSS, True))

            @pl.when(has_up)
            def _():
                act(send(me, zhalf, UP, True))

            @pl.when(has_down)
            def _():
                act(send(me, zhalf, DOWN, True))

    def forward(d, half, act):
        up, down = z + d, z - d

        @pl.when(up < n_z)
        def _():
            p = 2 * up + x
            if act is start:
                send(p, half, ACROSS).wait_recv()

            @pl.when(has_down)
            def _():
                act(send(p, half, DOWN))

            @pl.when((d > 1) | (half == 0))
            def _():
                act(send(p, half, ACROSS))

        @pl.when(down >= 0)
        def _():
            p = 2 * down + x
            if act is start:
                send(p, half, ACROSS).wait_recv()

            @pl.when(has_up)
            def _():
                act(send(p, half, UP))

            @pl.when((d > 1) | (half == 0))
            def _():
                act(send(p, half, ACROSS))

    def start(copy):
        copy.start()

    def drain(copy):
        copy.wait_send()

    own_sends(start)

    t = timestep[0]
    loads[0].wait()
    loads[1].wait()
    shift_row = mod_v[0, pl.ds(t, 1), :]
    scale_row = mod_v[1, pl.ds(t, 1), :]
    widened = tok_v[...].astype(jnp.float32)
    centred = widened - jnp.mean(widened, axis=-1, keepdims=True)
    variance = jnp.mean(centred * centred, axis=-1, keepdims=True)
    normed = centred * lax.rsqrt(variance + epsilon) * (1.0 + scale_row) + shift_row
    rows_v[core] = normed.astype(jnp.bfloat16)
    swap = pltpu.make_async_remote_copy(
        src_ref=rows_v.at[core], dst_ref=rows_v.at[core],
        send_sem=head_sem.at[0], recv_sem=head_sem.at[1],
        device_id={"head": 1 - core}, device_id_type=MESH,
    )
    swap.start()
    swap.wait_recv()

    rows = rows_v[...].reshape(patch_rows, rows_v.shape[2])
    for part in range(3):
        loads[2 + part].wait()
        mixed = jnp.dot(rows, w_v[part], preferred_element_type=jnp.float32)
        if part == 2:
            kv_v[1] = mixed.astype(jnp.bfloat16)
            continue
        gain = (q_gain if part == 0 else k_gain)[...]
        for h in range(heads):
            cols = slice(h * HD, (h + 1) * HD)
            scaled = rms_scaled(mixed[:, cols], gain)
            if part == 0:
                q_v[:, cols] = scaled
            else:
                kv_v[0, :, cols] = scaled
    store_kv = local(kv_v, new_kv, 6)
    store_kv.start()

    limit = length[0]
    lane = lax.broadcasted_iota(jnp.int32, (1, patch_rows), 1)

    def attend(keys, p, first):
        position = p * patch_rows + lane
        visible = ((position >= text_rows) | (position < limit)).astype(jnp.float32)
        for h in range(heads):
            cols = slice(h * HD, (h + 1) * HD)
            scores = lax.dot_general(
                q_v[:, cols], keys[0, :, cols], (((1,), (1,)), ((), ())),
                preferred_element_type=jnp.float32,
            ) * inverse_root
            exps = jnp.exp(scores) * visible
            part = jnp.dot(exps.astype(jnp.bfloat16), keys[1, :, cols],
                           preferred_element_type=jnp.float32)
            if first:
                den[h] = exps
                num[:, cols] = part
            else:
                den[h] += exps
                num[:, cols] += part

    def attend_far(p):
        attend(far.at[p], p, False)

    def attend_across(up_ok, p):
        @pl.when(up_ok)
        def _():
            send(p, 0, ACROSS).wait_recv()
            send(p, 1, ACROSS).wait_recv()
            attend_far(p)

    attend(kv_v, me, True)

    peer = 2 * z + xp
    send(peer, 1, ACROSS).wait_recv()

    @pl.when(z == n_z - 1)
    def _():
        send(peer, 1, DOWN).start()

    @pl.when(z == 0)
    def _():
        send(peer, 1, UP).start()

    def step(d, carry):
        up, down = z + d, z - d
        forward(d, 0, start)
        forward(d, 1, start)

        @pl.when((up == n_z - 1) & has_down)
        def _():
            send(peer, 1, DOWN).start()

        @pl.when((down == 0) & has_up)
        def _():
            send(peer, 1, UP).start()

        @pl.when(up < n_z)
        def _():
            attend_far(2 * up + x)

        @pl.when(down >= 0)
        def _():
            attend_far(2 * down + x)

        @pl.when(d == 1)
        def _():
            send(peer, 0, ACROSS).wait_recv()
            attend_far(peer)

        attend_across((d > 2) & (up - 1 < n_z), 2 * (up - 1) + xp)
        attend_across((d > 2) & (down + 1 >= 0), 2 * (down + 1) + xp)
        return carry

    lax.fori_loop(1, n_z, step, 0)
    if n_z > 2:
        attend_across(z == 0, 2 * (n_z - 1) + xp)
        attend_across(z == n_z - 1, xp)
    attend_across(has_up, 2 * (z + 1) + xp)
    attend_across(has_down, 2 * (z - 1) + xp)

    for h in range(heads):
        cols = slice(h * HD, (h + 1) * HD)
        total = jnp.sum(den[h], axis=-1, keepdims=True)
        merged = (num[:, cols] / total).astype(jnp.bfloat16)
        att[:, :, cols] = merged.reshape(2, tok_dev, HD)
    back = pltpu.make_async_remote_copy(
        src_ref=att.at[1 - core], dst_ref=att_in,
        send_sem=head_sem.at[2], recv_sem=head_sem.at[3],
        device_id={"head": 1 - core}, device_id_type=MESH,
    )
    back.start()
    loads[5].wait()
    mine = pl.ds(pl.multiple_of(core * width, width), width)
    theirs = pl.ds(pl.multiple_of((1 - core) * width, width), width)
    projected = jnp.dot(att[core], wo_v[mine, :], preferred_element_type=jnp.float32)
    back.wait_recv()
    projected += jnp.dot(att_in[...], wo_v[theirs, :], preferred_element_type=jnp.float32)
    update[...] = (mod_v[2, pl.ds(t, 1), :] * projected).astype(jnp.bfloat16)

    swap.wait_send()
    back.wait_send()
    store_kv.wait()
    own_sends(drain)

    @pl.when(has_up)
    def _():
        send(peer, 1, UP).wait_send()

    @pl.when(has_down)
    def _():
        send(peer, 1, DOWN).wait_send()

    def drain_step(d, carry):
        forward(d, 0, drain)
        forward(d, 1, drain)
        return carry

    lax.fori_loop(1, n_z, drain_step, 0)


def shards(n_patch, tokens, timestep, text_length, mod_table, w_qkv, q_gain, k_gain, w_out, stale_kv):
    tok_dev, model = tokens.shape
    rows = 2 * tok_dev
    width = w_qkv.shape[2]
    heads = width // HD
    bf, f32 = jnp.bfloat16, jnp.float32
    vmem, smem, anywhere = (pl.BlockSpec(memory_space=m) for m in (pltpu.VMEM, pltpu.SMEM, pl.ANY))
    mod = jnp.transpose(mod_table, (1, 0, 2))
    w = jnp.transpose(w_qkv, (1, 0, 2))

    def kernel(*refs):
        body(n_patch, *refs)

    return pl.pallas_call(
        kernel,
        out_shape=(
            jax.ShapeDtypeStruct((tok_dev, model), bf),
            jax.ShapeDtypeStruct((2, rows, width), bf),
        ),
        in_specs=[smem, smem, anywhere, anywhere, anywhere, vmem, vmem, anywhere, anywhere],
        out_specs=(vmem, anywhere),
        scratch_shapes=[
            pltpu.VMEM((tok_dev, model), bf),
            pltpu.VMEM(mod.shape, f32),
            pltpu.VMEM(w.shape, bf),
            pltpu.VMEM(w_out.shape, bf),
            pltpu.VMEM((2, tok_dev, model), bf),
            pltpu.VMEM((rows, width), bf),
            pltpu.VMEM((2, rows, width), bf),
            pltpu.VMEM((n_patch, 2, rows, width), bf),
            pltpu.VMEM((rows, width), f32),
            pltpu.VMEM((heads, rows, rows), f32),
            pltpu.VMEM((2, tok_dev, width), bf),
            pltpu.VMEM((tok_dev, width), bf),
            pltpu.SemaphoreType.DMA((7,)),
            pltpu.SemaphoreType.DMA((4,)),
            pltpu.SemaphoreType.DMA((3, n_patch, 2)),
            pltpu.SemaphoreType.DMA((n_patch, 2)),
        ],
        compiler_params=pltpu.CompilerParams(
            collective_id=0, has_side_effects=True, vmem_limit_bytes=52 * 1024 * 1024
        ),
    )(timestep, text_length, tokens, mod, w, q_gain.reshape(1, HD), k_gain.reshape(1, HD), w_out, stale_kv)


def solution(mesh):
    n_patch = mesh.shape["patch"]

    def local(*args):
        return shards(n_patch, *args)

    return jax.shard_map(
        local,
        mesh=mesh,
        in_specs=(
            P(("groups", "patch", "head"), None),
            P("groups"),
            P("groups"),
            P(),
            P(None, None, "head"),
            P(),
            P(),
            P(),
            P(None, ("groups", "patch"), "head"),
        ),
        out_specs=(P(("groups", "patch", "head"), None), P(None, ("groups", "patch"), "head")),
        check_vma=False,
    )
```

```python
import math

import jax
import jax.numpy as jnp
from jax import lax
from jax.experimental import pallas as pl
from jax.experimental.pallas import tpu as pltpu
from jax.sharding import PartitionSpec as P

HD = 128
epsilon = 1e-06
MESH = pl.DeviceIdType.MESH
ACROSS, DOWN, UP = 0, 1, 2


def rms_scaled(values, gain_vec):
    mean_square = jnp.mean(values * values, axis=-1, keepdims=True)
    return (values * lax.rsqrt(mean_square + epsilon) * gain_vec).astype(jnp.bfloat16)


def body(n_patch, timestep, length, tokens, mod, w_qkv, q_gain, k_gain, w_out, stale, update, new_kv,
         tok_v, mod_v, gain_v, w_v, wo_v, rows_v, fresh, kv_v, far, group, num, den, out_v, att,
         local_sem, head_sem, kv_send, kv_recv, fresh_send, fresh_recv, out_send, out_recv):
    tok_dev = tokens.shape[0]
    patch_rows = 2 * tok_dev
    width = w_qkv.shape[2]
    heads = width // HD
    per_col = heads // 2
    text_rows = 4 * patch_rows
    n_z = n_patch // 2
    inverse_root = 1.0 / math.sqrt(HD)

    me = lax.axis_index("patch")
    core = lax.axis_index("head")
    z, x = lax.div(me, 2), lax.rem(me, 2)
    xp = 1 - x
    level = lax.rem(z, 2)
    base = me - 2 * level - x
    slot = 2 * level + x
    peer = 2 * z + xp
    targets = {ACROSS: peer, DOWN: me - 2, UP: me + 2}

    def side(j, at_core):
        return (0, at_core, 1)[j]

    def goes_up(j):
        return (z < n_z - 1) & ((z < n_z - 2) | (side(j, core) == 1))

    def goes_down(j):
        return (z > 0) & ((z > 1) | (side(j, core) == 0))

    def owned(j):
        return level == side(j, core)

    def local(src, dst, at):
        return pltpu.make_async_copy(src, dst, local_sem.at[at])

    def head_cols(l):
        return pl.ds(pl.multiple_of(l * HD, HD), HD)

    loads = [local(tokens, tok_v, 0), local(mod, mod_v, 1)]
    loads += [local(w_qkv.at[i], w_v.at[i], 2 + i) for i in range(3)]
    loads += [local(w_out, wo_v, 5)]
    loads += [local(q_gain, gain_v.at[0], 7), local(k_gain, gain_v.at[1], 8)]
    loads += [local(stale.at[:, :, head_cols(3 * x + j)], far.at[me, j], 9 + j) for j in range(3)]
    for i in (0, 1, 6, 7, 2, 3, 4, 8, 9, 10, 5):
        loads[i].start()

    barrier = pltpu.get_barrier_semaphore()
    for s in range(4):
        for cc in range(2):
            @pl.when((slot != s) | (core != cc))
            def _(s=s, cc=cc):
                pl.semaphore_signal(barrier, inc=1, device_id={"patch": base + s, "head": cc},
                                    device_id_type=MESH)

    out_up = (level == 1) & (z < n_z - 1)
    out_down = (level == 0) & (z > 0)

    @pl.when(out_up)
    def _():
        pl.semaphore_signal(barrier, inc=1, device_id={"patch": me + 2}, device_id_type=MESH)

    @pl.when(out_down)
    def _():
        pl.semaphore_signal(barrier, inc=1, device_id={"patch": me - 2}, device_id_type=MESH)

    num[...] = jnp.zeros_like(num)
    den[...] = jnp.zeros_like(den)
    pl.semaphore_wait(barrier, 7 + out_up.astype(jnp.int32) + out_down.astype(jnp.int32))

    def send(p, j, way, src=None):
        return pltpu.make_async_remote_copy(
            src_ref=far.at[p, j] if src is None else src, dst_ref=far.at[p, j],
            send_sem=kv_send.at[way, p, j], recv_sem=kv_recv.at[p, j],
            device_id={"patch": targets[way]}, device_id_type=MESH,
        )

    def start(copy):
        copy.start()

    def drain(copy):
        copy.wait_send()

    def own_sends(act):
        for j in (0, 2, 1):
            act(send(me, j, ACROSS, stale.at[:, :, head_cols(3 * xp + j)]))
        for i in range(3):
            @pl.when(goes_up(2 - i))
            def _(j=2 - i):
                act(send(me, j, UP, stale.at[:, :, head_cols(3 * x + j)]))

            @pl.when(goes_down(i))
            def _(j=i):
                act(send(me, j, DOWN, stale.at[:, :, head_cols(3 * x + j)]))

    def peer_sends(act):
        for i in range(3):
            @pl.when(goes_up(2 - i))
            def _(j=2 - i):
                act(send(peer, j, UP))

            @pl.when(goes_down(i))
            def _(j=i):
                act(send(peer, j, DOWN))

    def forward(d, col, act):
        up, down = z + d, z - d
        for i in range(3):
            @pl.when((up < n_z) & ((z > 0) | (side(i, core) == 0)))
            def _(j=i):
                p = 2 * up + col
                if act is start:
                    send(p, j, ACROSS).wait_recv()

                @pl.when(goes_down(j))
                def _():
                    act(send(p, j, DOWN))

            @pl.when((down >= 0) & ((z < n_z - 1) | (side(2 - i, core) == 1)))
            def _(j=2 - i):
                p = 2 * down + col
                if act is start:
                    send(p, j, ACROSS).wait_recv()

                @pl.when(goes_up(j))
                def _():
                    act(send(p, j, UP))

    own_sends(start)

    t = timestep[0]
    loads[0].wait()
    loads[1].wait()
    shift_row = mod_v[0, pl.ds(t, 1), :]
    scale_row = mod_v[1, pl.ds(t, 1), :]
    widened = tok_v[...].astype(jnp.float32)
    centred = widened - jnp.mean(widened, axis=-1, keepdims=True)
    variance = jnp.mean(centred * centred, axis=-1, keepdims=True)
    normed = centred * lax.rsqrt(variance + epsilon) * (1.0 + scale_row) + shift_row
    rows_v[core] = normed.astype(jnp.bfloat16)
    swap = pltpu.make_async_remote_copy(
        src_ref=rows_v.at[core], dst_ref=rows_v.at[core],
        send_sem=head_sem.at[0], recv_sem=head_sem.at[1],
        device_id={"head": 1 - core}, device_id_type=MESH,
    )
    swap.start()
    swap.wait_recv()
    loads[6].wait()
    loads[7].wait()

    rows = rows_v[...].reshape(patch_rows, rows_v.shape[2])
    for part in range(3):
        loads[2 + part].wait()
        mixed = jnp.dot(rows, w_v[part], preferred_element_type=jnp.float32)
        for h in range(heads):
            cols = slice(h * HD, (h + 1) * HD)
            if part == 2:
                value = mixed[:, cols].astype(jnp.bfloat16)
            else:
                value = rms_scaled(mixed[:, cols], gain_v[part])
            fresh[h, part] = value
            if part > 0:
                kv_v[part - 1, :, cols] = value

    def fresh_copy(l):
        j = l % 3
        owner = base + 2 * side(j, core) + l // 3
        return pltpu.make_async_remote_copy(
            src_ref=fresh.at[l], dst_ref=group.at[j, slot],
            send_sem=fresh_send.at[l], recv_sem=fresh_recv.at[j, slot],
            device_id={"patch": owner}, device_id_type=MESH,
        )

    def fresh_here(l):
        return owned(l % 3) & (x == l // 3)

    def fresh_sends(act):
        for l in range(heads):
            @pl.when(jnp.logical_not(fresh_here(l)))
            def _(l=l):
                act(fresh_copy(l))

    fresh_sends(start)
    for l in range(heads):
        @pl.when(fresh_here(l))
        def _(l=l):
            group[l % 3, slot] = fresh[l]
    store_kv = local(kv_v, new_kv, 6)
    store_kv.start()

    for i in (0, 2, 1):
        send(peer, i, ACROSS).wait_recv()
    peer_sends(start)

    limit = length[0]
    lane = lax.broadcasted_iota(jnp.int32, (1, patch_rows), 1)
    all_rows = 4 * patch_rows
    row_slot = lax.div(lax.broadcasted_iota(jnp.int32, (all_rows, 1), 0), patch_rows)

    def seen(p):
        position = p * patch_rows + lane
        return (position >= text_rows) | (position < limit)

    def contract(queries, keys):
        return lax.dot_general(queries, keys, (((1,), (1,)), ((), ())),
                               preferred_element_type=jnp.float32) * inverse_root

    def attend(p):
        mask = seen(p) & (row_slot != p - base)

        def head(j):
            queries = group[j, :, 0].reshape(all_rows, HD)
            exps = jnp.where(mask, jnp.exp(contract(queries, far[p, j, 0])), 0.0)
            den[j] += exps
            num[j] += jnp.dot(exps.astype(jnp.bfloat16), far[p, j, 1],
                              preferred_element_type=jnp.float32)

        head(2 * level)

        @pl.when(owned(1))
        def _():
            head(1)

    def attend_fresh(j):
        for s in range(4):
            own = slice(s * patch_rows, (s + 1) * patch_rows)
            exps = jnp.where(seen(base + s), jnp.exp(contract(group[j, s, 0], group[j, s, 1])), 0.0)
            den[j, own] += exps
            num[j, own] += jnp.dot(exps.astype(jnp.bfloat16), group[j, s, 2],
                                   preferred_element_type=jnp.float32)

    def attend_level(d, col):
        @pl.when(z + d < n_z)
        def _():
            attend(2 * (z + d) + col)

        @pl.when(z - d >= 0)
        def _():
            attend(2 * (z - d) + col)

    forward(1, x, start)
    forward(1, xp, start)

    for j in range(3):
        loads[8 + j].wait()

        @pl.when(owned(j))
        def _(j=j):
            for s in range(4):
                @pl.when(slot != s)
                def _(s=s):
                    pltpu.make_async_remote_copy(
                        src_ref=group.at[j, s], dst_ref=group.at[j, s],
                        send_sem=fresh_send.at[j], recv_sem=fresh_recv.at[j, s],
                        device_id={"patch": peer}, device_id_type=MESH,
                    ).wait_recv()
            attend_fresh(j)

    attend(me)
    attend(peer)
    attend_level(1, x)

    def step(d, carry):
        forward(d, x, start)
        attend_level(d - 1, xp)
        forward(d, xp, start)
        attend_level(d, x)
        return carry

    lax.fori_loop(2, n_z, step, 0)
    attend_level(n_z - 1, xp)

    def out_copy(j, s, cc):
        return pltpu.make_async_remote_copy(
            src_ref=out_v.at[j, s, cc], dst_ref=att.at[:, head_cols(heads * core + 3 * x + j)],
            send_sem=out_send.at[j, s, cc], recv_sem=out_recv.at[heads * core + 3 * x + j],
            device_id={"patch": base + s, "head": cc}, device_id_type=MESH,
        )

    def out_sends(j, act):
        for s in range(4):
            for cc in range(2):
                @pl.when((slot != s) | (core != cc))
                def _(s=s, cc=cc):
                    act(out_copy(j, s, cc))

    for j in range(3):
        @pl.when(owned(j))
        def _(j=j):
            total = jnp.sum(den[j], axis=-1, keepdims=True)
            merged = (num[j] / total).astype(jnp.bfloat16)
            out_v[j] = merged.reshape(4, 2, tok_dev, HD)
            out_sends(j, start)
            att[:, head_cols(heads * core + 3 * x + j)] = out_v[j, slot, core]

    loads[5].wait()
    for g in range(2 * heads):
        l = g % heads
        at_core, col, j = g // heads, l // 3, l % 3
        here = (core == at_core) & (x == col) & (level == side(j, at_core))

        @pl.when(jnp.logical_not(here))
        def _(g=g):
            pltpu.make_async_remote_copy(
                src_ref=out_v.at[0, 0, 0], dst_ref=att.at[:, pl.ds(g * HD, HD)],
                send_sem=out_send.at[0, 0, 0], recv_sem=out_recv.at[g],
                device_id={"patch": peer}, device_id_type=MESH,
            ).wait_recv()

    projected = jnp.dot(att[...], wo_v[...], preferred_element_type=jnp.float32)
    update[...] = (mod_v[2, pl.ds(t, 1), :] * projected).astype(jnp.bfloat16)

    swap.wait_send()
    store_kv.wait()
    own_sends(drain)
    peer_sends(drain)
    fresh_sends(drain)
    for j in range(3):
        @pl.when(owned(j))
        def _(j=j):
            out_sends(j, drain)

    def drain_step(d, carry):
        forward(d, x, drain)
        forward(d, xp, drain)
        return carry

    lax.fori_loop(1, n_z, drain_step, 0)


def shards(n_patch, tokens, timestep, text_length, mod_table, w_qkv, q_gain, k_gain, w_out, stale_kv):
    tok_dev, model = tokens.shape
    rows = 2 * tok_dev
    width = w_qkv.shape[2]
    heads = width // HD
    bf, f32 = jnp.bfloat16, jnp.float32
    vmem, smem, anywhere = (pl.BlockSpec(memory_space=m) for m in (pltpu.VMEM, pltpu.SMEM, pl.ANY))
    mod = jnp.transpose(mod_table, (1, 0, 2))
    w = jnp.transpose(w_qkv, (1, 0, 2))

    def kernel(*refs):
        body(n_patch, *refs)

    dma = pltpu.SemaphoreType.DMA
    return pl.pallas_call(
        kernel,
        out_shape=(
            jax.ShapeDtypeStruct((tok_dev, model), bf),
            jax.ShapeDtypeStruct((2, rows, width), bf),
        ),
        in_specs=[smem, smem] + [anywhere] * 7,
        out_specs=(vmem, anywhere),
        scratch_shapes=[
            pltpu.VMEM((tok_dev, model), bf),
            pltpu.VMEM(mod.shape, f32),
            pltpu.VMEM((2, 1, HD), f32),
            pltpu.VMEM(w.shape, bf),
            pltpu.VMEM(w_out.shape, bf),
            pltpu.VMEM((2, tok_dev, model), bf),
            pltpu.VMEM((heads, 3, rows, HD), bf),
            pltpu.VMEM((2, rows, width), bf),
            pltpu.VMEM((n_patch, 3, 2, rows, HD), bf),
            pltpu.VMEM((3, 4, 3, rows, HD), bf),
            pltpu.VMEM((3, 4 * rows, HD), f32),
            pltpu.VMEM((3, 4 * rows, HD), f32),
            pltpu.VMEM((3, 4, 2, tok_dev, HD), bf),
            pltpu.VMEM((tok_dev, model), bf),
            dma((12,)),
            dma((2,)),
            dma((3, n_patch, 3)),
            dma((n_patch, 3)),
            dma((heads,)),
            dma((3, 4)),
            dma((3, 4, 2)),
            dma((2 * heads,)),
        ],
        compiler_params=pltpu.CompilerParams(
            collective_id=0, has_side_effects=True, vmem_limit_bytes=63 * 1024 * 1024
        ),
    )(timestep, text_length, tokens, mod, w, q_gain.reshape(1, HD), k_gain.reshape(1, HD), w_out, stale_kv)


def solution(mesh):
    n_patch = mesh.shape["patch"]

    def local(*args):
        return shards(n_patch, *args)

    return jax.shard_map(
        local,
        mesh=mesh,
        in_specs=(
            P(("groups", "patch", "head"), None),
            P("groups"),
            P("groups"),
            P(),
            P(None, None, "head"),
            P(),
            P(),
            P(),
            P(None, ("groups", "patch"), "head"),
        ),
        out_specs=(P(("groups", "patch", "head"), None), P(None, ("groups", "patch"), "head")),
        check_vma=False,
    )
```

```python
import math

import jax
import jax.numpy as jnp
from jax import lax
from jax.experimental import pallas as pl
from jax.experimental.pallas import tpu as pltpu
from jax.sharding import PartitionSpec as P

HD = 128
epsilon = 1e-06
MESH = pl.DeviceIdType.MESH
ACROSS, DOWN, UP = 0, 1, 2


def rms_scaled(values, gain_vec):
    mean_square = jnp.mean(values * values, axis=-1, keepdims=True)
    return (values * lax.rsqrt(mean_square + epsilon) * gain_vec).astype(jnp.bfloat16)


def body(n_patch, timestep, length, tokens, mod, w_qkv, q_gain, k_gain, w_out, stale, update, new_kv,
         tok_v, mod_v, gain_v, w_v, wo_v, rows_v, fresh, kv_v, far, group, num, den, out_v, att,
         local_sem, head_sem, kv_send, kv_recv, fresh_send, fresh_recv, out_send, out_recv):
    tok_dev = tokens.shape[0]
    patch_rows = 2 * tok_dev
    width = w_qkv.shape[2]
    heads = width // HD
    per_col = heads // 2
    text_rows = 4 * patch_rows
    n_z = n_patch // 2
    inverse_root = 1.0 / math.sqrt(HD)

    me = lax.axis_index("patch")
    core = lax.axis_index("head")
    z, x = lax.div(me, 2), lax.rem(me, 2)
    xp = 1 - x
    level = lax.rem(z, 2)
    base = me - 2 * level - x
    slot = 2 * level + x
    peer = 2 * z + xp
    targets = {ACROSS: peer, DOWN: me - 2, UP: me + 2}

    def side(j, at_core):
        return (0, at_core, 1)[j]

    def goes_up(j):
        return (z < n_z - 1) & ((z < n_z - 2) | (side(j, core) == 1))

    def goes_down(j):
        return (z > 0) & ((z > 1) | (side(j, core) == 0))

    def owned(j):
        return level == side(j, core)

    def local(src, dst, at):
        return pltpu.make_async_copy(src, dst, local_sem.at[at])

    def head_cols(l):
        return pl.ds(pl.multiple_of(l * HD, HD), HD)

    loads = [local(tokens, tok_v, 0), local(mod, mod_v, 1)]
    loads += [local(w_qkv.at[i], w_v.at[i], 2 + i) for i in range(3)]
    loads += [local(w_out, wo_v, 5)]
    loads += [local(q_gain, gain_v.at[0], 7), local(k_gain, gain_v.at[1], 8)]
    loads += [local(stale.at[:, :, head_cols(3 * x + j)], far.at[me, j], 9 + j) for j in range(3)]
    for i in (0, 1, 6, 7, 2, 3, 4, 8, 9, 10, 5):
        loads[i].start()

    barrier = pltpu.get_barrier_semaphore()
    for s in range(4):
        for cc in range(2):
            @pl.when((slot != s) | (core != cc))
            def _(s=s, cc=cc):
                pl.semaphore_signal(barrier, inc=1, device_id={"patch": base + s, "head": cc},
                                    device_id_type=MESH)

    out_up = (level == 1) & (z < n_z - 1)
    out_down = (level == 0) & (z > 0)

    @pl.when(out_up)
    def _():
        pl.semaphore_signal(barrier, inc=1, device_id={"patch": me + 2}, device_id_type=MESH)

    @pl.when(out_down)
    def _():
        pl.semaphore_signal(barrier, inc=1, device_id={"patch": me - 2}, device_id_type=MESH)

    num[...] = jnp.zeros_like(num)
    den[...] = jnp.zeros_like(den)
    pl.semaphore_wait(barrier, 7 + out_up.astype(jnp.int32) + out_down.astype(jnp.int32))

    def send(p, j, way, src=None):
        return pltpu.make_async_remote_copy(
            src_ref=far.at[p, j] if src is None else src, dst_ref=far.at[p, j],
            send_sem=kv_send.at[way, p, j], recv_sem=kv_recv.at[p, j],
            device_id={"patch": targets[way]}, device_id_type=MESH,
        )

    def start(copy):
        copy.start()

    def drain(copy):
        copy.wait_send()

    def own_sends(act):
        for j in (0, 2, 1):
            act(send(me, j, ACROSS, stale.at[:, :, head_cols(3 * xp + j)]))
        for i in range(3):
            @pl.when(goes_up(2 - i))
            def _(j=2 - i):
                act(send(me, j, UP, stale.at[:, :, head_cols(3 * x + j)]))

            @pl.when(goes_down(i))
            def _(j=i):
                act(send(me, j, DOWN, stale.at[:, :, head_cols(3 * x + j)]))

    def peer_sends(act):
        for i in range(3):
            @pl.when(goes_up(2 - i))
            def _(j=2 - i):
                act(send(peer, j, UP))

            @pl.when(goes_down(i))
            def _(j=i):
                act(send(peer, j, DOWN))

    def forward(d, col, act):
        up, down = z + d, z - d
        for i in range(3):
            @pl.when((up < n_z) & ((z > 0) | (side(i, core) == 0)))
            def _(j=i):
                p = 2 * up + col
                if act is start:
                    send(p, j, ACROSS).wait_recv()

                @pl.when(goes_down(j))
                def _():
                    act(send(p, j, DOWN))

            @pl.when((down >= 0) & ((z < n_z - 1) | (side(2 - i, core) == 1)))
            def _(j=2 - i):
                p = 2 * down + col
                if act is start:
                    send(p, j, ACROSS).wait_recv()

                @pl.when(goes_up(j))
                def _():
                    act(send(p, j, UP))

    own_sends(start)

    t = timestep[0]
    loads[0].wait()
    loads[1].wait()
    shift_row = mod_v[0, pl.ds(t, 1), :]
    scale_row = mod_v[1, pl.ds(t, 1), :]
    widened = tok_v[...].astype(jnp.float32)
    centred = widened - jnp.mean(widened, axis=-1, keepdims=True)
    variance = jnp.mean(centred * centred, axis=-1, keepdims=True)
    normed = centred * lax.rsqrt(variance + epsilon) * (1.0 + scale_row) + shift_row
    rows_v[core] = normed.astype(jnp.bfloat16)
    swap = pltpu.make_async_remote_copy(
        src_ref=rows_v.at[core], dst_ref=rows_v.at[core],
        send_sem=head_sem.at[0], recv_sem=head_sem.at[1],
        device_id={"head": 1 - core}, device_id_type=MESH,
    )
    swap.start()
    swap.wait_recv()
    loads[6].wait()
    loads[7].wait()

    rows = rows_v[...].reshape(patch_rows, rows_v.shape[2])
    for part in range(3):
        loads[2 + part].wait()
        mixed = jnp.dot(rows, w_v[part], preferred_element_type=jnp.float32)
        for h in range(heads):
            cols = slice(h * HD, (h + 1) * HD)
            if part == 2:
                value = mixed[:, cols].astype(jnp.bfloat16)
            else:
                value = rms_scaled(mixed[:, cols], gain_v[part])
            fresh[h, part] = value
            if part > 0:
                kv_v[part - 1, :, cols] = value

    def fresh_copy(l):
        j = l % 3
        owner = base + 2 * side(j, core) + l // 3
        return pltpu.make_async_remote_copy(
            src_ref=fresh.at[l], dst_ref=group.at[j, slot],
            send_sem=fresh_send.at[l], recv_sem=fresh_recv.at[j, slot],
            device_id={"patch": owner}, device_id_type=MESH,
        )

    def fresh_here(l):
        return owned(l % 3) & (x == l // 3)

    def fresh_sends(act):
        for l in range(heads):
            @pl.when(jnp.logical_not(fresh_here(l)))
            def _(l=l):
                act(fresh_copy(l))

    fresh_sends(start)
    for l in range(heads):
        @pl.when(fresh_here(l))
        def _(l=l):
            group[l % 3, slot] = fresh[l]
    store_kv = local(kv_v, new_kv, 6)
    store_kv.start()

    for i in (0, 2, 1):
        send(peer, i, ACROSS).wait_recv()
    peer_sends(start)

    limit = length[0]
    lane = lax.broadcasted_iota(jnp.int32, (1, patch_rows), 1)
    all_rows = 4 * patch_rows
    row_slot = lax.div(lax.broadcasted_iota(jnp.int32, (all_rows, 1), 0), patch_rows)

    def seen(p):
        position = p * patch_rows + lane
        return (position >= text_rows) | (position < limit)

    def contract(queries, keys):
        return lax.dot_general(queries, keys, (((1,), (1,)), ((), ())),
                               preferred_element_type=jnp.float32) * inverse_root

    def attend(p):
        mask = seen(p) & (row_slot != p - base)

        def head(j):
            queries = group[j, :, 0].reshape(all_rows, HD)
            exps = jnp.where(mask, jnp.exp(contract(queries, far[p, j, 0])), 0.0)
            den[j] += exps
            num[j] += jnp.dot(exps.astype(jnp.bfloat16), far[p, j, 1],
                              preferred_element_type=jnp.float32)

        head(2 * level)

        @pl.when(owned(1))
        def _():
            head(1)

    def attend_fresh(j):
        for s in range(4):
            own = slice(s * patch_rows, (s + 1) * patch_rows)
            exps = jnp.where(seen(base + s), jnp.exp(contract(group[j, s, 0], group[j, s, 1])), 0.0)
            den[j, own] += exps
            num[j, own] += jnp.dot(exps.astype(jnp.bfloat16), group[j, s, 2],
                                   preferred_element_type=jnp.float32)

    def attend_level(d, col):
        @pl.when(z + d < n_z)
        def _():
            attend(2 * (z + d) + col)

        @pl.when(z - d >= 0)
        def _():
            attend(2 * (z - d) + col)

    forward(1, x, start)
    forward(1, xp, start)
    if n_z > 2:
        forward(2, x, start)

    for j in range(3):
        loads[8 + j].wait()

        @pl.when(owned(j))
        def _(j=j):
            for s in range(4):
                @pl.when(slot != s)
                def _(s=s):
                    pltpu.make_async_remote_copy(
                        src_ref=group.at[j, s], dst_ref=group.at[j, s],
                        send_sem=fresh_send.at[j], recv_sem=fresh_recv.at[j, s],
                        device_id={"patch": peer}, device_id_type=MESH,
                    ).wait_recv()
            attend_fresh(j)

    attend(me)
    attend(peer)
    attend_level(1, x)

    if n_z > 2:
        forward(2, xp, start)
        attend_level(1, xp)
        attend_level(2, x)

    def step(d, carry):
        forward(d, x, start)
        attend_level(d - 1, xp)
        forward(d, xp, start)
        attend_level(d, x)
        return carry

    lax.fori_loop(3, n_z, step, 0)
    attend_level(n_z - 1, xp)

    def out_copy(j, s, cc):
        return pltpu.make_async_remote_copy(
            src_ref=out_v.at[j, s, cc], dst_ref=att.at[:, head_cols(heads * core + 3 * x + j)],
            send_sem=out_send.at[j, s, cc], recv_sem=out_recv.at[heads * core + 3 * x + j],
            device_id={"patch": base + s, "head": cc}, device_id_type=MESH,
        )

    def out_sends(j, act):
        for s in range(4):
            for cc in range(2):
                @pl.when((slot != s) | (core != cc))
                def _(s=s, cc=cc):
                    act(out_copy(j, s, cc))

    for j in range(3):
        @pl.when(owned(j))
        def _(j=j):
            total = jnp.sum(den[j], axis=-1, keepdims=True)
            merged = (num[j] / total).astype(jnp.bfloat16)
            out_v[j] = merged.reshape(4, 2, tok_dev, HD)
            out_sends(j, start)
            att[:, head_cols(heads * core + 3 * x + j)] = out_v[j, slot, core]

    swap.wait_send()
    store_kv.wait()
    own_sends(drain)
    peer_sends(drain)
    fresh_sends(drain)
    def drain_step(d, carry):
        forward(d, x, drain)
        forward(d, xp, drain)
        return carry

    lax.fori_loop(1, n_z, drain_step, 0)

    loads[5].wait()
    for g in range(2 * heads):
        l = g % heads
        at_core, col, j = g // heads, l // 3, l % 3
        here = (core == at_core) & (x == col) & (level == side(j, at_core))

        @pl.when(jnp.logical_not(here))
        def _(g=g):
            pltpu.make_async_remote_copy(
                src_ref=out_v.at[0, 0, 0], dst_ref=att.at[:, pl.ds(g * HD, HD)],
                send_sem=out_send.at[0, 0, 0], recv_sem=out_recv.at[g],
                device_id={"patch": peer}, device_id_type=MESH,
            ).wait_recv()

    projected = jnp.dot(att[...], wo_v[...], preferred_element_type=jnp.float32)
    update[...] = (mod_v[2, pl.ds(t, 1), :] * projected).astype(jnp.bfloat16)

    for j in range(3):
        @pl.when(owned(j))
        def _(j=j):
            out_sends(j, drain)


def deliver(update, new_kv, update_out, new_kv_out, sem):
    copies = [pltpu.make_async_copy(update, update_out, sem.at[0]),
              pltpu.make_async_copy(new_kv, new_kv_out, sem.at[1])]
    for copy in copies:
        copy.start()
    for copy in copies:
        copy.wait()


def shards(n_patch, tokens, timestep, text_length, mod_table, w_qkv, q_gain, k_gain, w_out, stale_kv):
    tok_dev, model = tokens.shape
    rows = 2 * tok_dev
    width = w_qkv.shape[2]
    heads = width // HD
    bf, f32 = jnp.bfloat16, jnp.float32
    vmem, smem, anywhere = (pl.BlockSpec(memory_space=m) for m in (pltpu.VMEM, pltpu.SMEM, pl.ANY))
    mod = jnp.transpose(mod_table, (1, 0, 2))
    w = jnp.transpose(w_qkv, (1, 0, 2))

    def kernel(*refs):
        body(n_patch, *refs)

    dma = pltpu.SemaphoreType.DMA
    results = pl.pallas_call(
        kernel,
        out_shape=(
            jax.ShapeDtypeStruct((tok_dev, model), bf),
            jax.ShapeDtypeStruct((2, rows, width), bf),
        ),
        in_specs=[smem, smem] + [anywhere] * 7,
        out_specs=(vmem, anywhere),
        scratch_shapes=[
            pltpu.VMEM((tok_dev, model), bf),
            pltpu.VMEM(mod.shape, f32),
            pltpu.VMEM((2, 1, HD), f32),
            pltpu.VMEM(w.shape, bf),
            pltpu.VMEM(w_out.shape, bf),
            pltpu.VMEM((2, tok_dev, model), bf),
            pltpu.VMEM((heads, 3, rows, HD), bf),
            pltpu.VMEM((2, rows, width), bf),
            pltpu.VMEM((n_patch, 3, 2, rows, HD), bf),
            pltpu.VMEM((3, 4, 3, rows, HD), bf),
            pltpu.VMEM((3, 4 * rows, HD), f32),
            pltpu.VMEM((3, 4 * rows, HD), f32),
            pltpu.VMEM((3, 4, 2, tok_dev, HD), bf),
            pltpu.VMEM((tok_dev, model), bf),
            dma((12,)),
            dma((2,)),
            dma((3, n_patch, 3)),
            dma((n_patch, 3)),
            dma((heads,)),
            dma((3, 4)),
            dma((3, 4, 2)),
            dma((2 * heads,)),
        ],
        compiler_params=pltpu.CompilerParams(
            collective_id=0, has_side_effects=True, vmem_limit_bytes=63 * 1024 * 1024
        ),
    )(timestep, text_length, tokens, mod, w, q_gain.reshape(1, HD), k_gain.reshape(1, HD), w_out, stale_kv)
    return pl.pallas_call(
        deliver,
        out_shape=tuple(jax.ShapeDtypeStruct(r.shape, r.dtype) for r in results),
        in_specs=[anywhere] * 2,
        out_specs=(anywhere, anywhere),
        scratch_shapes=[dma((2,))],
    )(*results)


def solution(mesh):
    n_patch = mesh.shape["patch"]

    def local(*args):
        return shards(n_patch, *args)

    return jax.shard_map(
        local,
        mesh=mesh,
        in_specs=(
            P(("groups", "patch", "head"), None),
            P("groups"),
            P("groups"),
            P(),
            P(None, None, "head"),
            P(),
            P(),
            P(),
            P(None, ("groups", "patch"), "head"),
        ),
        out_specs=(P(("groups", "patch", "head"), None), P(None, ("groups", "patch"), "head")),
        check_vma=False,
    )
```

```python
import math

import jax
import jax.numpy as jnp
from jax import lax
from jax.experimental import pallas as pl
from jax.experimental.pallas import tpu as pltpu
from jax.sharding import PartitionSpec as P

HD = 128
epsilon = 1e-06
MESH = pl.DeviceIdType.MESH
ACROSS, DOWN, UP = 0, 1, 2


def rms_scaled(values, gain_vec):
    mean_square = jnp.mean(values * values, axis=-1, keepdims=True)
    return (values * lax.rsqrt(mean_square + epsilon) * gain_vec).astype(jnp.bfloat16)


def body(n_patch, timestep, length, tokens, mod, w_qkv, q_gain, k_gain, w_out, stale, update, new_kv,
         tok_v, mod_v, gain_v, w_v, wo_v, rows_v, fresh, kv_v, far, group, num, den, out_v, att,
         local_sem, head_sem, kv_send, kv_recv, fresh_send, fresh_recv, out_send, out_recv):
    tok_dev = tokens.shape[0]
    patch_rows = 2 * tok_dev
    width = w_qkv.shape[2]
    heads = width // HD
    per_col = heads // 2
    text_rows = 4 * patch_rows
    n_z = n_patch // 2
    inverse_root = 1.0 / math.sqrt(HD)

    me = lax.axis_index("patch")
    core = lax.axis_index("head")
    z, x = lax.div(me, 2), lax.rem(me, 2)
    xp = 1 - x
    level = lax.rem(z, 2)
    base = me - 2 * level - x
    slot = 2 * level + x
    peer = 2 * z + xp
    targets = {ACROSS: peer, DOWN: me - 2, UP: me + 2}

    def side(j, at_core):
        return (0, at_core, 1)[j]

    def goes_up(j):
        return (z < n_z - 1) & ((z < n_z - 2) | (side(j, core) == 1))

    def goes_down(j):
        return (z > 0) & ((z > 1) | (side(j, core) == 0))

    def owned(j):
        return level == side(j, core)

    def local(src, dst, at):
        return pltpu.make_async_copy(src, dst, local_sem.at[at])

    def head_cols(l):
        return pl.ds(pl.multiple_of(l * HD, HD), HD)

    loads = [local(tokens, tok_v, 0), local(mod, mod_v, 1)]
    loads += [local(w_qkv.at[i], w_v.at[i], 2 + i) for i in range(3)]
    loads += [local(w_out, wo_v, 5)]
    loads += [local(q_gain, gain_v.at[0], 7), local(k_gain, gain_v.at[1], 8)]
    loads += [local(stale.at[:, :, head_cols(3 * x + j)], far.at[me, j], 9 + j) for j in range(3)]
    for i in (0, 1, 6, 7, 2, 3, 4, 8, 9, 10, 5):
        loads[i].start()

    barrier = pltpu.get_barrier_semaphore()
    for s in range(4):
        for cc in range(2):
            @pl.when((slot != s) | (core != cc))
            def _(s=s, cc=cc):
                pl.semaphore_signal(barrier, inc=1, device_id={"patch": base + s, "head": cc},
                                    device_id_type=MESH)

    out_up = (level == 1) & (z < n_z - 1)
    out_down = (level == 0) & (z > 0)

    @pl.when(out_up)
    def _():
        pl.semaphore_signal(barrier, inc=1, device_id={"patch": me + 2}, device_id_type=MESH)

    @pl.when(out_down)
    def _():
        pl.semaphore_signal(barrier, inc=1, device_id={"patch": me - 2}, device_id_type=MESH)

    num[...] = jnp.zeros_like(num)
    den[...] = jnp.zeros_like(den)
    pl.semaphore_wait(barrier, 7 + out_up.astype(jnp.int32) + out_down.astype(jnp.int32))

    def send(p, j, way, src=None):
        return pltpu.make_async_remote_copy(
            src_ref=far.at[p, j] if src is None else src, dst_ref=far.at[p, j],
            send_sem=kv_send.at[way, p, j], recv_sem=kv_recv.at[p, j],
            device_id={"patch": targets[way]}, device_id_type=MESH,
        )

    def start(copy):
        copy.start()

    def drain(copy):
        copy.wait_send()

    def own_sends(act):
        for j in (0, 2, 1):
            act(send(me, j, ACROSS, stale.at[:, :, head_cols(3 * xp + j)]))
        for i in range(3):
            @pl.when(goes_up(2 - i))
            def _(j=2 - i):
                act(send(me, j, UP, stale.at[:, :, head_cols(3 * x + j)]))

            @pl.when(goes_down(i))
            def _(j=i):
                act(send(me, j, DOWN, stale.at[:, :, head_cols(3 * x + j)]))

    def peer_sends(act):
        for i in range(3):
            @pl.when(goes_up(2 - i))
            def _(j=2 - i):
                act(send(peer, j, UP))

            @pl.when(goes_down(i))
            def _(j=i):
                act(send(peer, j, DOWN))

    def forward(d, col, act):
        up, down = z + d, z - d
        for i in range(3):
            @pl.when((up < n_z) & ((z > 0) | (side(i, core) == 0)))
            def _(j=i):
                p = 2 * up + col
                if act is start:
                    send(p, j, ACROSS).wait_recv()

                @pl.when(goes_down(j))
                def _():
                    act(send(p, j, DOWN))

            @pl.when((down >= 0) & ((z < n_z - 1) | (side(2 - i, core) == 1)))
            def _(j=2 - i):
                p = 2 * down + col
                if act is start:
                    send(p, j, ACROSS).wait_recv()

                @pl.when(goes_up(j))
                def _():
                    act(send(p, j, UP))

    own_sends(start)

    t = timestep[0]
    loads[0].wait()
    loads[1].wait()
    shift_row = mod_v[0, pl.ds(t, 1), :]
    scale_row = mod_v[1, pl.ds(t, 1), :]
    widened = tok_v[...].astype(jnp.float32)
    centred = widened - jnp.mean(widened, axis=-1, keepdims=True)
    variance = jnp.mean(centred * centred, axis=-1, keepdims=True)
    normed = centred * lax.rsqrt(variance + epsilon) * (1.0 + scale_row) + shift_row
    rows_v[core] = normed.astype(jnp.bfloat16)
    swap = pltpu.make_async_remote_copy(
        src_ref=rows_v.at[core], dst_ref=rows_v.at[core],
        send_sem=head_sem.at[0], recv_sem=head_sem.at[1],
        device_id={"head": 1 - core}, device_id_type=MESH,
    )
    swap.start()
    swap.wait_recv()
    loads[6].wait()
    loads[7].wait()

    rows = rows_v[...].reshape(patch_rows, rows_v.shape[2])
    for part in range(3):
        loads[2 + part].wait()
        mixed = jnp.dot(rows, w_v[part], preferred_element_type=jnp.float32)
        for h in range(heads):
            cols = slice(h * HD, (h + 1) * HD)
            if part == 2:
                value = mixed[:, cols].astype(jnp.bfloat16)
            else:
                value = rms_scaled(mixed[:, cols], gain_v[part])
            fresh[h, part] = value
            if part > 0:
                kv_v[part - 1, :, cols] = value

    def fresh_copy(l):
        j = l % 3
        owner = base + 2 * side(j, core) + l // 3
        return pltpu.make_async_remote_copy(
            src_ref=fresh.at[l], dst_ref=group.at[j, slot],
            send_sem=fresh_send.at[l], recv_sem=fresh_recv.at[j, slot],
            device_id={"patch": owner}, device_id_type=MESH,
        )

    def fresh_here(l):
        return owned(l % 3) & (x == l // 3)

    def fresh_sends(act):
        for l in range(heads):
            @pl.when(jnp.logical_not(fresh_here(l)))
            def _(l=l):
                act(fresh_copy(l))

    fresh_sends(start)
    for l in range(heads):
        @pl.when(fresh_here(l))
        def _(l=l):
            group[l % 3, slot] = fresh[l]
    store_kv = local(kv_v, new_kv, 6)
    store_kv.start()

    for i in (0, 2, 1):
        send(peer, i, ACROSS).wait_recv()
    peer_sends(start)

    limit = length[0]
    lane = lax.broadcasted_iota(jnp.int32, (1, patch_rows), 1)
    all_rows = 4 * patch_rows
    row_slot = lax.div(lax.broadcasted_iota(jnp.int32, (all_rows, 1), 0), patch_rows)

    def seen(p):
        position = p * patch_rows + lane
        return (position >= text_rows) | (position < limit)

    def contract(queries, keys):
        return lax.dot_general(queries, keys, (((1,), (1,)), ((), ())),
                               preferred_element_type=jnp.float32) * inverse_root

    def attend(p):
        mask = seen(p) & (row_slot != p - base)

        def head(j):
            queries = group[j, :, 0].reshape(all_rows, HD)
            exps = jnp.where(mask, jnp.exp(contract(queries, far[p, j, 0])), 0.0)
            den[j] += exps
            num[j] += jnp.dot(exps.astype(jnp.bfloat16), far[p, j, 1],
                              preferred_element_type=jnp.float32)

        head(2 * level)

        @pl.when(owned(1))
        def _():
            head(1)

    def attend_fresh(j):
        for s in range(4):
            own = slice(s * patch_rows, (s + 1) * patch_rows)
            exps = jnp.where(seen(base + s), jnp.exp(contract(group[j, s, 0], group[j, s, 1])), 0.0)
            den[j, own] += exps
            num[j, own] += jnp.dot(exps.astype(jnp.bfloat16), group[j, s, 2],
                                   preferred_element_type=jnp.float32)

    def attend_level(d, col):
        @pl.when(z + d < n_z)
        def _():
            attend(2 * (z + d) + col)

        @pl.when(z - d >= 0)
        def _():
            attend(2 * (z - d) + col)

    forward(1, x, start)
    forward(1, xp, start)
    if n_z > 2:
        forward(2, x, start)

    for j in range(3):
        loads[8 + j].wait()

        @pl.when(owned(j))
        def _(j=j):
            for s in range(4):
                @pl.when(slot != s)
                def _(s=s):
                    pltpu.make_async_remote_copy(
                        src_ref=group.at[j, s], dst_ref=group.at[j, s],
                        send_sem=fresh_send.at[j], recv_sem=fresh_recv.at[j, s],
                        device_id={"patch": peer}, device_id_type=MESH,
                    ).wait_recv()
            attend_fresh(j)

    attend(me)
    attend(peer)
    attend_level(1, x)

    if n_z > 2:
        forward(2, xp, start)
        attend_level(1, xp)
        attend_level(2, x)

    def step(d, carry):
        forward(d, x, start)
        attend_level(d - 1, xp)
        forward(d, xp, start)
        attend_level(d, x)
        return carry

    lax.fori_loop(3, n_z, step, 0)
    attend_level(n_z - 1, xp)

    def out_copy(j, s, cc):
        return pltpu.make_async_remote_copy(
            src_ref=out_v.at[j, s, cc], dst_ref=att.at[:, head_cols(heads * core + 3 * x + j)],
            send_sem=out_send.at[j, s, cc], recv_sem=out_recv.at[heads * core + 3 * x + j],
            device_id={"patch": base + s, "head": cc}, device_id_type=MESH,
        )

    def out_sends(j, act):
        for s in range(4):
            for cc in range(2):
                @pl.when((slot != s) | (core != cc))
                def _(s=s, cc=cc):
                    act(out_copy(j, s, cc))

    for j in range(3):
        @pl.when(owned(j))
        def _(j=j):
            total = jnp.sum(den[j], axis=-1, keepdims=True)
            merged = (num[j] / total).astype(jnp.bfloat16)
            out_v[j] = merged.reshape(4, 2, tok_dev, HD)
            out_sends(j, start)
            att[:, head_cols(heads * core + 3 * x + j)] = out_v[j, slot, core]

    swap.wait_send()
    store_kv.wait()
    own_sends(drain)
    peer_sends(drain)
    fresh_sends(drain)
    def drain_step(d, carry):
        forward(d, x, drain)
        forward(d, xp, drain)
        return carry

    lax.fori_loop(1, n_z, drain_step, 0)

    loads[5].wait()
    for g in range(2 * heads):
        l = g % heads
        at_core, col, j = g // heads, l // 3, l % 3
        here = (core == at_core) & (x == col) & (level == side(j, at_core))

        @pl.when(jnp.logical_not(here))
        def _(g=g):
            pltpu.make_async_remote_copy(
                src_ref=out_v.at[0, 0, 0], dst_ref=att.at[:, pl.ds(g * HD, HD)],
                send_sem=out_send.at[0, 0, 0], recv_sem=out_recv.at[g],
                device_id={"patch": peer}, device_id_type=MESH,
            ).wait_recv()

    projected = jnp.dot(att[...], wo_v[...], preferred_element_type=jnp.float32)
    update[...] = (mod_v[2, pl.ds(t, 1), :] * projected).astype(jnp.bfloat16)

    for j in range(3):
        @pl.when(owned(j))
        def _(j=j):
            out_sends(j, drain)


def deliver(update, new_kv, update_out, new_kv_out, update_v, kv_v, sem):
    reads = [pltpu.make_async_copy(update, update_v, sem.at[0]),
             pltpu.make_async_copy(new_kv, kv_v, sem.at[1])]
    writes = [pltpu.make_async_copy(update_v, update_out, sem.at[2]),
              pltpu.make_async_copy(kv_v, new_kv_out, sem.at[3])]
    for read in reads:
        read.start()
    for read, write in zip(reads, writes):
        read.wait()
        write.start()
    for write in writes:
        write.wait()


def shards(n_patch, tokens, timestep, text_length, mod_table, w_qkv, q_gain, k_gain, w_out, stale_kv):
    tok_dev, model = tokens.shape
    rows = 2 * tok_dev
    width = w_qkv.shape[2]
    heads = width // HD
    bf, f32 = jnp.bfloat16, jnp.float32
    vmem, smem, anywhere = (pl.BlockSpec(memory_space=m) for m in (pltpu.VMEM, pltpu.SMEM, pl.ANY))
    mod = jnp.transpose(mod_table, (1, 0, 2))
    w = jnp.transpose(w_qkv, (1, 0, 2))

    def kernel(*refs):
        body(n_patch, *refs)

    dma = pltpu.SemaphoreType.DMA
    results = pl.pallas_call(
        kernel,
        out_shape=(
            jax.ShapeDtypeStruct((tok_dev, model), bf),
            jax.ShapeDtypeStruct((2, rows, width), bf),
        ),
        in_specs=[smem, smem] + [anywhere] * 7,
        out_specs=(vmem, anywhere),
        scratch_shapes=[
            pltpu.VMEM((tok_dev, model), bf),
            pltpu.VMEM(mod.shape, f32),
            pltpu.VMEM((2, 1, HD), f32),
            pltpu.VMEM(w.shape, bf),
            pltpu.VMEM(w_out.shape, bf),
            pltpu.VMEM((2, tok_dev, model), bf),
            pltpu.VMEM((heads, 3, rows, HD), bf),
            pltpu.VMEM((2, rows, width), bf),
            pltpu.VMEM((n_patch, 3, 2, rows, HD), bf),
            pltpu.VMEM((3, 4, 3, rows, HD), bf),
            pltpu.VMEM((3, 4 * rows, HD), f32),
            pltpu.VMEM((3, 4 * rows, HD), f32),
            pltpu.VMEM((3, 4, 2, tok_dev, HD), bf),
            pltpu.VMEM((tok_dev, model), bf),
            dma((12,)),
            dma((2,)),
            dma((3, n_patch, 3)),
            dma((n_patch, 3)),
            dma((heads,)),
            dma((3, 4)),
            dma((3, 4, 2)),
            dma((2 * heads,)),
        ],
        compiler_params=pltpu.CompilerParams(
            collective_id=0, has_side_effects=True, vmem_limit_bytes=63 * 1024 * 1024
        ),
    )(timestep, text_length, tokens, mod, w, q_gain.reshape(1, HD), k_gain.reshape(1, HD), w_out, stale_kv)
    return pl.pallas_call(
        deliver,
        out_shape=tuple(jax.ShapeDtypeStruct(r.shape, r.dtype) for r in results),
        in_specs=[anywhere] * 2,
        out_specs=(anywhere, anywhere),
        scratch_shapes=[pltpu.VMEM(r.shape, r.dtype) for r in results] + [dma((4,))],
    )(*results)


def solution(mesh):
    n_patch = mesh.shape["patch"]

    def local(*args):
        return shards(n_patch, *args)

    return jax.shard_map(
        local,
        mesh=mesh,
        in_specs=(
            P(("groups", "patch", "head"), None),
            P("groups"),
            P("groups"),
            P(),
            P(None, None, "head"),
            P(),
            P(),
            P(),
            P(None, ("groups", "patch"), "head"),
        ),
        out_specs=(P(("groups", "patch", "head"), None), P(None, ("groups", "patch"), "head")),
        check_vma=False,
    )
```
